32 devices in a mesh: ctx: 8 (over y, x, core), section: 4 (over z).
Axes of the slice: x: 2, y: 2, z: 4, core: 2. Of those that a mesh axis runs over, the one named last changes fastest.
Arguments:
- queries: bfloat16 [4, 1024, 4096], P('section', 'ctx'), may hold values from -24 to 24
- keys: bfloat16 [4, 1024, 512], P('section', 'ctx'), may hold values from -24 to 24
- values: bfloat16 [4, 1024, 512], P('section', 'ctx'), may hold values from -6 to 6
- doc_lengths: int32 [4, 4], P('section'), may hold values from 1 to 512, 1024 in all within a row
- interp_num: int32 [1], replicated, may hold values from 250 to 999
- interp_den: int32 [1], replicated, may hold values from 1000 to 1999
Outputs:
- handed: bfloat16 [4, 1024, 4096], P('section', 'ctx')
The draws below stay inside these ranges and needn't reach their ends.
Inputs may be any that keep to these rules, and one draw needn't show every extreme that they name: `doc_lengths`: each row sums to 1024; its longest document has exactly 512 tokens.
All inputs are finite; a program needn't handle non-finite values.
Results may differ from the reference program's by a relative error of at most 0.0099.
Values may be sent and summed in bfloat16 or wider, within the bound.
A program may use at most 64 MiB of HBM per device.

```python
import math
import jax
import jax.numpy as jnp
import numpy as np
from jax import lax

QUERY_HEADS = 32
KEY_VALUE_HEADS = 4
HEAD_DIMENSION = 128
TOK_DEV = 128
DOCS = 4
SPAN = 64
SEQUENCE_TOKENS = 1024
RELAY_SECTIONS = 4
N_CTX = 8


def random_base_sample(key, heads, salt):
    shape = (RELAY_SECTIONS, SEQUENCE_TOKENS, heads, HEAD_DIMENSION)
    return jnp.clip(jax.random.normal(jax.random.fold_in(key, salt), shape, jnp.float32), -6.0, 6.0)


def draw_queries(key, part):
    input_array = random_base_sample(key, QUERY_HEADS, 11)
    return input_array.reshape(RELAY_SECTIONS, SEQUENCE_TOKENS, QUERY_HEADS * HEAD_DIMENSION).astype(jnp.bfloat16)


def draw_keys(key, part):
    input_array = random_base_sample(key, KEY_VALUE_HEADS, 23)
    return input_array.reshape(RELAY_SECTIONS, SEQUENCE_TOKENS, KEY_VALUE_HEADS * HEAD_DIMENSION).astype(jnp.bfloat16)


def block_levels(key, shape, split, least, largest):
    def one(axis_at, shards_of):
        draws = jax.random.uniform(jax.random.fold_in(jax.random.fold_in(key, 6), axis_at), (shards_of,), jnp.float32, least / len(split), largest / len(split))
        return jnp.repeat(jnp.exp(draws), shape[axis_at] // shards_of).reshape((-1,) + (1,) * (len(shape) - axis_at - 1))

    factor_of = one(*split[0])
    for cut in split[1:]:
        factor_of = factor_of * one(*cut)
    return factor_of


def length_profile(number_of, total, reach, slope):
    weights = [(1 << 20) // math.isqrt(standing ** slope) + 1 for standing in range(2, number_of + 1)]
    spare, given = total - reach - (number_of - 1), [1] * (number_of - 1)
    while spare > 0:
        free = [i for i in range(number_of - 1) if given[i] < reach]
        whole, remaining = sum([weights[i] for i in free]), spare
        for i in free:
            addition = min(reach - given[i], max(1, remaining * weights[i] // whole), spare)
            given[i] = given[i] + addition
            spare = spare - addition
    return np.array([reach] + given)


def uneven_parts(stream_key, count, total, reach, lean):
    if count == 2:
        one = jax.random.randint(stream_key, (), max(1, total - reach), min(reach, total - 1) + 1)
        return jnp.stack([one, total - one])
    sizes = jnp.asarray(length_profile(count, total, reach, lean), jnp.int32)
    twos = (count - 1) // 2
    giver, sink = sizes[1:1 + 2 * twos:2], sizes[2:2 + 2 * twos:2]
    margin = jnp.minimum(giver - 1, reach - sink)
    moved = jax.random.randint(jax.random.fold_in(stream_key, 1), (twos,), 0, 1 << 20) % (margin + 1)
    sizes = sizes.at[1:1 + 2 * twos:2].set(giver - moved).at[2:2 + 2 * twos:2].set(sink + moved)
    return sizes[jax.random.permutation(jax.random.fold_in(stream_key, 2), count)]


def centred(rng, shape, deviation, reach, shards=(), kind=jnp.bfloat16):
    result = jax.random.normal(rng, shape, jnp.float32) * deviation
    if len(shards) > 0:
        result = block_levels(rng, shape, shards, -0.22, 0.18) * result
    return jnp.clip(result, min=-reach, max=reach).astype(kind)


def setup_inputs(seed: int = 0) -> dict:
    splits = jax.random.split(jax.random.key(seed), 7)
    queries = draw_queries(jax.random.fold_in(splits[6], 71), 0)
    keys = draw_keys(jax.random.fold_in(splits[6], 71), 0)
    values = centred(splits[2], (RELAY_SECTIONS, SEQUENCE_TOKENS, KEY_VALUE_HEADS * HEAD_DIMENSION), 1.0, 6.0, ((0, 4), (1, 8)))
    doc_lengths = jax.vmap(lambda own: uneven_parts(own, DOCS, SEQUENCE_TOKENS, SEQUENCE_TOKENS // 2, 2))(jax.random.split(splits[3], RELAY_SECTIONS)).reshape((RELAY_SECTIONS, DOCS)).astype(jnp.int32)
    interp_num = jax.random.randint(splits[4], (1,), 250, 1000).astype(jnp.int32)
    interp_den = jax.random.randint(splits[5], (1,), 1000, 2000).astype(jnp.int32)
    return {"queries": queries, "keys": keys, "values": values, "doc_lengths": doc_lengths, "interp_num": interp_num, "interp_den": interp_den}


THETA = 500000.0
document_masked_scores = -1e+30

def document_info(positions, lengths):
    doc_ends = jnp.cumsum(lengths).astype(jnp.int32)
    passed = positions[:, None] >= doc_ends[None, :]
    doc_ids = lax.optimization_barrier(jnp.sum(passed.astype(jnp.int32), axis=1)).astype(jnp.int32)
    starts = lax.optimization_barrier(jnp.sum(jnp.where(passed, lengths[None, :], 0), axis=1)).astype(jnp.int32)
    return (doc_ids, (positions - starts).astype(jnp.int32))

def rotation_tables(input_array, position_starts, stretch_factor):
    half_size = HEAD_DIMENSION // 2
    inverse_freq = THETA ** (-(2.0 * jnp.arange(half_size, dtype=jnp.float32)) / HEAD_DIMENSION)
    angles = position_starts.astype(jnp.float32)[:, None] * stretch_factor * inverse_freq[None, :]
    cosine = jnp.cos(angles)[:, None, :]
    sine = jnp.sin(angles)[:, None, :]
    widened = input_array.astype(jnp.float32)
    first_half = widened[..., :half_size]
    second_half = widened[..., half_size:]
    joined = jnp.concatenate([first_half * cosine - second_half * sine, second_half * cosine + first_half * sine], axis=-1)
    return joined.astype(jnp.bfloat16)

def fold_positions(rows):
    shard = rows // TOK_DEV
    within = rows % TOK_DEV
    return jnp.where(within < SPAN, shard * SPAN + within, (2 * N_CTX - 1 - shard) * SPAN + within - SPAN).astype(jnp.int32)

def unfold_rows(positions):
    block_number = positions // SPAN
    within = positions % SPAN
    return jnp.where(block_number < N_CTX, block_number * TOK_DEV + within, (2 * N_CTX - 1 - block_number) * TOK_DEV + SPAN + within).astype(jnp.int32)

def reference(queries, keys, values, doc_lengths, interp_num, interp_den):
    stretch_factor = interp_num[0].astype(jnp.float32) / interp_den[0].astype(jnp.float32)
    query_group_width = QUERY_HEADS // KEY_VALUE_HEADS
    score_scale = 1.0 / math.sqrt(HEAD_DIMENSION)
    sequence = jnp.arange(SEQUENCE_TOKENS, dtype=jnp.int32)
    sequence_row_count = unfold_rows(sequence)
    folded_pos = fold_positions(sequence)
    block_rows = min(512, SEQUENCE_TOKENS)

    def one_section(inputs):
        queries_per_section, keys_per_section, values_per_section, lengths = inputs
        doc_ids, position_starts = document_info(sequence, lengths)
        turned_queries = rotation_tables(queries_per_section[sequence_row_count].reshape(SEQUENCE_TOKENS, QUERY_HEADS, HEAD_DIMENSION), position_starts, stretch_factor).reshape(SEQUENCE_TOKENS, KEY_VALUE_HEADS, query_group_width, HEAD_DIMENSION)
        turned_keys = rotation_tables(keys_per_section[sequence_row_count].reshape(SEQUENCE_TOKENS, KEY_VALUE_HEADS, HEAD_DIMENSION), position_starts, stretch_factor)
        sorted_value_rows = values_per_section[sequence_row_count].reshape(SEQUENCE_TOKENS, KEY_VALUE_HEADS, HEAD_DIMENSION)
        outputs = []
        for block_number in range(SEQUENCE_TOKENS // block_rows):
            low_row = block_number * block_rows
            high_row = low_row + block_rows
            query_block = turned_queries[low_row:high_row].astype(jnp.float32)
            current_key_block = turned_keys[:high_row].astype(jnp.float32)
            scores = jnp.einsum('qhgd,khd->qhgk', query_block, current_key_block) * score_scale
            allowed = (sequence[:high_row][None, :] <= sequence[low_row:high_row][:, None]) & (doc_ids[:high_row][None, :] == doc_ids[low_row:high_row][:, None])
            scores = jnp.where(allowed[:, None, None, :], scores, document_masked_scores)
            weights = jax.nn.softmax(scores, axis=-1).astype(jnp.bfloat16)
            attended = jnp.einsum('qhgk,khd->qhgd', weights.astype(jnp.float32), sorted_value_rows[:high_row].astype(jnp.float32))
            outputs.append(attended.astype(jnp.bfloat16).reshape(block_rows, QUERY_HEADS * HEAD_DIMENSION))
        in_order = jnp.concatenate(outputs, axis=0)
        return in_order[folded_pos]
    attended_all = lax.map(one_section, (queries, keys, values, doc_lengths))
    return jnp.roll(attended_all, 1, axis=0)
```

```python
from functools import partial
import math

import jax
import jax.numpy as jnp
from jax import lax
from jax.experimental import pallas as pl
from jax.experimental.pallas import tpu as pltpu
from jax.sharding import PartitionSpec as P

HEADS = 32
KV = 4
D = 128
GROUP = HEADS // KV
STACK = 4
SUBS = GROUP // STACK
THETA = 500000.0
MASKED = -1e30
SCALE = math.log2(math.e) / math.sqrt(D)
MESH = pl.DeviceIdType.MESH


def kernel(
    n, sections, q_ref, k_ref, v_ref, len_ref, num_ref, den_ref, out_ref,
    kv, cos_ref, sin_ref, bias_e, bias_l, obuf,
    send_sem, recv_sem, osend_sem, orecv_sem,
):
    me = lax.axis_index("ctx")
    sec = lax.axis_index("section")
    nxt = lax.rem(sec + 1, sections)
    prv = lax.rem(sec + sections - 1, sections)
    chips = n // 2
    chip, core = me // 2, me % 2
    partner = chip * 2 + 1 - core
    rows = q_ref.shape[1]
    half = rows // 2

    def peer(d):
        return lax.rem(chip + d, chips) * 2 + core

    barrier = pltpu.get_barrier_semaphore()
    for d in range(1, chips):
        pl.semaphore_signal(barrier, inc=1, device_id={"ctx": peer(d)}, device_id_type=MESH)
    pl.semaphore_signal(barrier, inc=1, device_id={"ctx": partner}, device_id_type=MESH)
    pl.semaphore_signal(barrier, inc=1, device_id={"section": nxt}, device_id_type=MESH)
    pl.semaphore_signal(barrier, inc=1, device_id={"section": prv}, device_id_type=MESH)

    r = lax.broadcasted_iota(jnp.int32, (rows, D), 0)
    pos = jnp.where(r < half, me * half + r, (2 * n - 1 - me) * half + r - half)
    start = jnp.zeros_like(pos)
    end = jnp.int32(0)
    for d in range(len_ref.shape[1]):
        length = len_ref[0, d]
        end = end + length
        start = start + jnp.where(pos >= end, length, 0)
    ratio = jnp.full((rows, D), num_ref[0], jnp.int32).astype(jnp.float32) / jnp.full(
        (rows, D), den_ref[0], jnp.int32
    ).astype(jnp.float32)
    lane = lax.broadcasted_iota(jnp.int32, (rows, D), 1)
    k_index = jnp.where(lane < D // 2, lane, lane - D // 2).astype(jnp.float32)
    freq = jnp.exp(k_index * (-2.0 / D * math.log(THETA)))
    angle = (pos - start).astype(jnp.float32) * ratio * freq
    cos = jnp.cos(angle)
    sin = jnp.where(lane < D // 2, -1.0, 1.0) * jnp.sin(angle)
    cos_ref[...] = cos
    sin_ref[...] = sin

    def rotate(x, c, s):
        x = x.astype(jnp.float32)
        return (x * c + pltpu.roll(x, D // 2, 1) * s).astype(jnp.bfloat16)

    def copy(h, shard, slot, to):
        return pltpu.make_async_remote_copy(
            src_ref=kv.at[h, shard],
            dst_ref=kv.at[h, shard],
            send_sem=send_sem.at[h, slot],
            recv_sem=recv_sem.at[h, shard],
            device_id={"ctx": to},
            device_id_type=MESH,
        )

    for h in range(KV):
        cols = slice(h * D, (h + 1) * D)
        kv[h, me, :, :D] = rotate(k_ref[0, :, cols], cos, sin)
        kv[h, me, :, D:] = v_ref[0, :, cols]
    pl.semaphore_wait(barrier, chips + 2)

    def push(h, _):
        for d in range(1, chips):
            copy(h, me, d, peer(d)).start()
        copy(h, me, 0, partner).start()
        return 0

    lax.fori_loop(0, KV, push, 0)

    def forward(h):
        for d in range(1, chips):
            shard = peer(chips - d)
            copy(h, shard, chips + d, partner).wait_recv()
            copy(h, shard, chips + d, partner).start()

    keys = n * half
    index = lax.broadcasted_iota(jnp.int32, (rows, keys), 1)
    q_pos, q_start = pos[:, :1], start[:, :1]
    bias_e[...] = jnp.where((index <= q_pos) & (index >= q_start), 0.0, MASKED)
    index = lax.broadcasted_iota(jnp.int32, (half, keys), 1)
    late = (2 * n - 1) * half + lax.rem(index, half) - lax.div(index, half) * half
    bias_l[...] = jnp.where((late <= q_pos[half:]) & (late >= q_start[half:]), 0.0, MASKED)

    forward(0)

    def out_copy(h, sub):
        cols = pl.ds(pl.multiple_of((h * SUBS + sub) * STACK * D, D), STACK * D)
        return pltpu.make_async_remote_copy(
            src_ref=obuf.at[:, cols],
            dst_ref=out_ref.at[0, :, cols],
            send_sem=osend_sem.at[h, sub],
            recv_sem=orecv_sem.at[h, sub],
            device_id={"section": nxt},
            device_id_type=MESH,
        )

    def attend(h, sub):
        c, s = cos_ref[...], sin_ref[...]
        base = (h * SUBS + sub) * STACK * D
        heads = [
            rotate(q_ref[0, :, pl.ds(pl.multiple_of(base + g * D, D), D)], c, s)
            for g in range(STACK)
        ]
        early_kv, late_kv = kv[h, :, :half, :], kv[h, :, half:, :]
        ke = early_kv[:, :, :D].reshape(keys, D)
        kl = late_kv[:, :, :D].reshape(keys, D)
        ones = jnp.ones((keys, D), jnp.bfloat16)
        ve = jnp.concatenate([early_kv[:, :, D:].reshape(keys, D), ones], axis=1)
        vl = jnp.concatenate([late_kv[:, :, D:].reshape(keys, D), ones], axis=1)
        dims = (((1,), (1,)), ((), ()))
        qa = jnp.concatenate(heads, axis=0)
        ql = jnp.concatenate([x[half:] for x in heads], axis=0)
        se = lax.dot_general(qa, ke, dims, preferred_element_type=jnp.float32)
        sl = lax.dot_general(ql, kl, dims, preferred_element_type=jnp.float32)
        se = se.reshape(STACK, rows, keys) + bias_e[...][None]
        sl = sl.reshape(STACK, half, keys) + bias_l[...][None]
        me_ = jnp.max(se, axis=-1, keepdims=True)
        ml = jnp.maximum(jnp.max(sl, axis=-1, keepdims=True), me_[:, half:])
        ma = jnp.concatenate([me_[:, :half], ml], axis=1)
        pe = jnp.exp2((se - ma) * SCALE).astype(jnp.bfloat16).reshape(STACK * rows, keys)
        pL = jnp.exp2((sl - ml) * SCALE).astype(jnp.bfloat16).reshape(STACK * half, keys)
        ae = jnp.dot(pe, ve, preferred_element_type=jnp.float32).reshape(STACK, rows, 2 * D)
        al = jnp.dot(pL, vl, preferred_element_type=jnp.float32).reshape(STACK, half, 2 * D)
        for g in range(STACK):
            cols = pl.ds(pl.multiple_of(base + g * D, D), D)
            top = ae[g, :half]
            low = ae[g, half:] + al[g]
            obuf[:half, cols] = (top[:, :D] / top[:, D:]).astype(jnp.bfloat16)
            obuf[half:, cols] = (low[:, :D] / low[:, D:]).astype(jnp.bfloat16)
        out_copy(h, sub).start()

    def head(h, _):
        for d in range(chips):
            shard = lax.rem(chip + d, chips) * 2 + 1 - core
            copy(h, shard, 0, partner).wait_recv()
        attend(h, 0)

        @pl.when(h + 1 < KV)
        def _():
            forward(h + 1)

        for sub in range(1, SUBS):
            attend(h, sub)
        return 0

    lax.fori_loop(0, KV, head, 0)

    def finish(h, _):
        for d in range(2 * chips):
            if d != chips:
                copy(h, me, d, partner).wait_send()
        for sub in range(SUBS):
            out_copy(h, sub).wait_send()
            out_copy(h, sub).wait_recv()
        return 0

    lax.fori_loop(0, KV, finish, 0)


def solution(mesh):
    n, sections = mesh.shape["ctx"], mesh.shape["section"]

    def on_device(queries, keys, values, doc_lengths, interp_num, interp_den):
        rows = queries.shape[1]
        half = rows // 2
        vmem = pl.BlockSpec(memory_space=pltpu.VMEM)
        smem = pl.BlockSpec(memory_space=pltpu.SMEM)
        return pl.pallas_call(
            partial(kernel, n, sections),
            out_shape=jax.ShapeDtypeStruct(queries.shape, jnp.bfloat16),
            in_specs=[vmem, vmem, vmem, smem, smem, smem],
            out_specs=pl.BlockSpec(memory_space=pl.ANY),
            scratch_shapes=[
                pltpu.VMEM((KV, n, rows, 2 * D), jnp.bfloat16),
                pltpu.VMEM((rows, D), jnp.float32),
                pltpu.VMEM((rows, D), jnp.float32),
                pltpu.VMEM((rows, n * half), jnp.float32),
                pltpu.VMEM((half, n * half), jnp.float32),
                pltpu.VMEM((rows, HEADS * D), jnp.bfloat16),
                pltpu.SemaphoreType.DMA((KV, n)),
                pltpu.SemaphoreType.DMA((KV, n)),
                pltpu.SemaphoreType.DMA((KV, SUBS)),
                pltpu.SemaphoreType.DMA((KV, SUBS)),
            ],
            compiler_params=pltpu.CompilerParams(
                collective_id=0, has_side_effects=True, vmem_limit_bytes=56 * 1024 * 1024
            ),
        )(queries, keys, values, doc_lengths, interp_num, interp_den)

    tokens = P("section", "ctx", None)
    return jax.shard_map(
        on_device,
        mesh=mesh,
        in_specs=(tokens, tokens, tokens, P("section", None), P(), P()),
        out_specs=tokens,
        check_vma=False,
    )
```

```python
from functools import partial
import math

import jax
import jax.numpy as jnp
from jax import lax
from jax.experimental import pallas as pl
from jax.experimental.pallas import tpu as pltpu
from jax.sharding import PartitionSpec as P

HEADS = 32
KV = 4
D = 128
GROUP = HEADS // KV
STACK = 4
SUBS = GROUP // STACK
THETA = 500000.0
MASKED = -1e30
SCALE = math.log2(math.e) / math.sqrt(D)
MESH = pl.DeviceIdType.MESH


def kernel(
    n, sections, q_hbm, k_hbm, v_hbm, len_ref, num_ref, den_ref, out_ref,
    kv, cos_ref, sin_ref, bias_e, bias_l, obuf,
    qbuf, kbuf, vbuf, kv_give, q_give, q_take, len_give, len_take,
    send_sem, recv_sem, osend_sem, orecv_sem, zsend_sem, zrecv_sem, load_sem, store_sem,
):
    me = lax.axis_index("ctx")
    sec = lax.axis_index("section")
    nxt = lax.rem(sec + 1, sections)
    prv = lax.rem(sec + sections - 1, sections)
    chips = n // 2
    chip, core = me // 2, me % 2
    partner = chip * 2 + 1 - core
    rows = qbuf.shape[0]
    half = rows // 2
    last = (KV - 1) * GROUP * D

    loads = [
        pltpu.make_async_copy(k_hbm.at[0], kbuf, load_sem.at[0]),
        pltpu.make_async_copy(v_hbm.at[0], vbuf, load_sem.at[1]),
        pltpu.make_async_copy(
            q_hbm.at[0, :, last:], qbuf.at[:, last:], load_sem.at[2]
        ),
        pltpu.make_async_copy(
            q_hbm.at[0, :, :last], qbuf.at[:, :last], load_sem.at[3]
        ),
    ]
    for load in loads:
        load.start()

    def peer(d):
        return lax.rem(chip + d, chips) * 2 + core

    barrier = pltpu.get_barrier_semaphore()
    for d in range(1, chips):
        pl.semaphore_signal(barrier, inc=1, device_id={"ctx": peer(d)}, device_id_type=MESH)
    pl.semaphore_signal(barrier, inc=1, device_id={"ctx": partner}, device_id_type=MESH)
    pl.semaphore_signal(barrier, inc=1, device_id={"section": nxt}, device_id_type=MESH)
    pl.semaphore_signal(barrier, inc=1, device_id={"section": prv}, device_id_type=MESH)

    r = lax.broadcasted_iota(jnp.int32, (rows, D), 0)
    pos = jnp.where(r < half, me * half + r, (2 * n - 1 - me) * half + r - half)
    def starts(lengths):
        begin = jnp.zeros_like(pos)
        end = jnp.zeros((1, D), jnp.int32)
        for length in lengths:
            end = end + length
            begin = begin + jnp.where(pos >= end, length, 0)
        return begin

    docs = len_ref.shape[1]
    for d in range(docs):
        len_give[d : d + 1, :] = jnp.full((1, D), len_ref[0, d], jnp.int32)
    start = starts([len_give[d : d + 1, :] for d in range(docs)])
    ratio = jnp.full((rows, D), num_ref[0], jnp.int32).astype(jnp.float32) / jnp.full(
        (rows, D), den_ref[0], jnp.int32
    ).astype(jnp.float32)
    lane = lax.broadcasted_iota(jnp.int32, (rows, D), 1)
    k_index = jnp.where(lane < D // 2, lane, lane - D // 2).astype(jnp.float32)
    freq = jnp.exp(k_index * (-2.0 / D * math.log(THETA)))
    angle = (pos - start).astype(jnp.float32) * ratio * freq
    cos = jnp.cos(angle)
    sin = jnp.where(lane < D // 2, -1.0, 1.0) * jnp.sin(angle)
    cos_ref[...] = cos
    sin_ref[...] = sin

    def rotate(x, c, s):
        x = x.astype(jnp.float32)
        return (x * c + pltpu.roll(x, D // 2, 1) * s).astype(jnp.bfloat16)

    def copy(h, shard, slot, to):
        return pltpu.make_async_remote_copy(
            src_ref=kv.at[h, shard],
            dst_ref=kv.at[h, shard],
            send_sem=send_sem.at[h, slot],
            recv_sem=recv_sem.at[h, shard],
            device_id={"ctx": to},
            device_id_type=MESH,
        )

    zpairs = [(kv_give, kv.at[KV - 1, me]), (len_give, len_take)]
    for sub in range(SUBS):
        zpairs.append((q_give.at[sub], q_take.at[sub]))
    zcopies = [
        pltpu.make_async_remote_copy(
            src_ref=src,
            dst_ref=dst,
            send_sem=zsend_sem.at[i],
            recv_sem=zrecv_sem.at[i],
            device_id={"section": nxt},
            device_id_type=MESH,
        )
        for i, (src, dst) in enumerate(zpairs)
    ]

    def push(h):
        for d in range(1, chips):
            copy(h, me, d, peer(d)).start()
        copy(h, me, 0, partner).start()

    loads[0].wait()
    loads[1].wait()
    for h in range(KV):
        cols = slice(h * D, (h + 1) * D)
        turned = rotate(kbuf[:, cols], cos, sin)
        if h == KV - 1:
            kv_give[:, :D] = turned
            kv_give[:, D:] = vbuf[:, cols]
        else:
            kv[h, me, :, :D] = turned
            kv[h, me, :, D:] = vbuf[:, cols]
    pl.semaphore_wait(barrier, chips + 2)
    zcopies[0].start()
    zcopies[1].start()
    push(0)
    loads[2].wait()
    for sub in range(SUBS):
        for g in range(STACK):
            at = last + (sub * STACK + g) * D
            q_give[sub, :, g * D : (g + 1) * D] = rotate(qbuf[:, at : at + D], cos, sin)
        zcopies[2 + sub].start()
    for h in range(1, KV - 1):
        push(h)

    def forward(h):
        for d in range(1, chips):
            shard = peer(chips - d)
            copy(h, shard, chips + d, partner).wait_recv()
            copy(h, shard, chips + d, partner).start()

    keys = n * half

    def set_bias(begin):
        q_pos, q_start = pos[:, :1], begin[:, :1]
        index = lax.broadcasted_iota(jnp.int32, (rows, keys), 1)
        bias_e[...] = jnp.where((index <= q_pos) & (index >= q_start), 0.0, MASKED)
        index = lax.broadcasted_iota(jnp.int32, (half, keys), 1)
        late = (2 * n - 1) * half + lax.rem(index, half) - lax.div(index, half) * half
        seen = (late <= q_pos[half:]) & (late >= q_start[half:])
        bias_l[...] = jnp.where(seen, 0.0, MASKED)

    set_bias(start)
    loads[3].wait()
    forward(0)

    def out_copy(h, sub):
        cols = pl.ds(pl.multiple_of((h * SUBS + sub) * STACK * D, D), STACK * D)
        return pltpu.make_async_remote_copy(
            src_ref=obuf.at[:, cols],
            dst_ref=out_ref.at[0, :, cols],
            send_sem=osend_sem.at[h, sub],
            recv_sem=orecv_sem.at[h, sub],
            device_id={"section": nxt},
            device_id_type=MESH,
        )

    def own_heads(h, sub):
        c, s = cos_ref[...], sin_ref[...]
        base = (h * SUBS + sub) * STACK * D
        return [
            rotate(qbuf[:, pl.ds(pl.multiple_of(base + g * D, D), D)], c, s)
            for g in range(STACK)
        ]

    def attend(h, sub, heads):
        base = (h * SUBS + sub) * STACK * D
        early_kv, late_kv = kv[h, :, :half, :], kv[h, :, half:, :]
        ke = early_kv[:, :, :D].reshape(keys, D)
        kl = late_kv[:, :, :D].reshape(keys, D)
        ones = jnp.ones((keys, D), jnp.bfloat16)
        ve = jnp.concatenate([early_kv[:, :, D:].reshape(keys, D), ones], axis=1)
        vl = jnp.concatenate([late_kv[:, :, D:].reshape(keys, D), ones], axis=1)
        dims = (((1,), (1,)), ((), ()))
        qa = jnp.concatenate(heads, axis=0)
        ql = jnp.concatenate([x[half:] for x in heads], axis=0)
        se = lax.dot_general(qa, ke, dims, preferred_element_type=jnp.float32)
        sl = lax.dot_general(ql, kl, dims, preferred_element_type=jnp.float32)
        se = se.reshape(STACK, rows, keys) + bias_e[...][None]
        sl = sl.reshape(STACK, half, keys) + bias_l[...][None]
        me_ = jnp.max(se, axis=-1, keepdims=True)
        ml = jnp.maximum(jnp.max(sl, axis=-1, keepdims=True), me_[:, half:])
        ma = jnp.concatenate([me_[:, :half], ml], axis=1)
        pe = jnp.exp2((se - ma) * SCALE).astype(jnp.bfloat16).reshape(STACK * rows, keys)
        pL = jnp.exp2((sl - ml) * SCALE).astype(jnp.bfloat16).reshape(STACK * half, keys)
        ae = jnp.dot(pe, ve, preferred_element_type=jnp.float32).reshape(STACK, rows, 2 * D)
        al = jnp.dot(pL, vl, preferred_element_type=jnp.float32).reshape(STACK, half, 2 * D)
        for g in range(STACK):
            cols = pl.ds(pl.multiple_of(base + g * D, D), D)
            top = ae[g, :half]
            low = ae[g, half:] + al[g]
            obuf[:half, cols] = (top[:, :D] / top[:, D:]).astype(jnp.bfloat16)
            obuf[half:, cols] = (low[:, :D] / low[:, D:]).astype(jnp.bfloat16)

    def from_partner(h):
        for d in range(chips):
            shard = lax.rem(chip + d, chips) * 2 + 1 - core
            copy(h, shard, 0, partner).wait_recv()

    def head(h, _):
        from_partner(h)
        attend(h, 0, own_heads(h, 0))
        out_copy(h, 0).start()

        @pl.when(h == 0)
        def _():
            zcopies[0].wait_recv()
            push(KV - 1)

        forward(h + 1)
        for sub in range(1, SUBS):
            attend(h, sub, own_heads(h, sub))
            out_copy(h, sub).start()
        return 0

    lax.fori_loop(0, KV - 1, head, 0)

    zcopies[1].wait_recv()
    set_bias(starts([len_take[d : d + 1, :] for d in range(docs)]))
    from_partner(KV - 1)
    stores = []
    for sub in range(SUBS):
        zcopies[2 + sub].wait_recv()
        heads = [q_take[sub, :, g * D : (g + 1) * D] for g in range(STACK)]
        attend(KV - 1, sub, heads)
        at = last + sub * STACK * D
        cols = slice(at, at + STACK * D)
        store = pltpu.make_async_copy(obuf.at[:, cols], out_ref.at[0, :, cols], store_sem.at[sub])
        store.start()
        stores.append(store)

    def finish(h, _):
        for d in range(2 * chips):
            if d != chips:
                copy(h, me, d, partner).wait_send()
        return 0

    lax.fori_loop(0, KV, finish, 0)
    for store in stores:
        store.wait()
    for zcopy in zcopies:
        zcopy.wait_send()

    def arrive(h, _):
        for sub in range(SUBS):
            out_copy(h, sub).wait_send()
            out_copy(h, sub).wait_recv()
        return 0

    lax.fori_loop(0, KV - 1, arrive, 0)


def solution(mesh):
    n, sections = mesh.shape["ctx"], mesh.shape["section"]

    def on_device(queries, keys, values, doc_lengths, interp_num, interp_den):
        rows = queries.shape[1]
        half = rows // 2
        docs = doc_lengths.shape[1]
        hbm = pl.BlockSpec(memory_space=pltpu.HBM)
        smem = pl.BlockSpec(memory_space=pltpu.SMEM)
        return pl.pallas_call(
            partial(kernel, n, sections),
            out_shape=jax.ShapeDtypeStruct(queries.shape, jnp.bfloat16),
            in_specs=[hbm, hbm, hbm, smem, smem, smem],
            out_specs=pl.BlockSpec(memory_space=pl.ANY),
            scratch_shapes=[
                pltpu.VMEM((KV, n, rows, 2 * D), jnp.bfloat16),
                pltpu.VMEM((rows, D), jnp.float32),
                pltpu.VMEM((rows, D), jnp.float32),
                pltpu.VMEM((rows, n * half), jnp.float32),
                pltpu.VMEM((half, n * half), jnp.float32),
                pltpu.VMEM((rows, HEADS * D), jnp.bfloat16),
                pltpu.VMEM((rows, HEADS * D), jnp.bfloat16),
                pltpu.VMEM((rows, KV * D), jnp.bfloat16),
                pltpu.VMEM((rows, KV * D), jnp.bfloat16),
                pltpu.VMEM((rows, 2 * D), jnp.bfloat16),
                pltpu.VMEM((SUBS, rows, STACK * D), jnp.bfloat16),
                pltpu.VMEM((SUBS, rows, STACK * D), jnp.bfloat16),
                pltpu.VMEM((docs, D), jnp.int32),
                pltpu.VMEM((docs, D), jnp.int32),
                pltpu.SemaphoreType.DMA((KV, n)),
                pltpu.SemaphoreType.DMA((KV, n)),
                pltpu.SemaphoreType.DMA((KV, SUBS)),
                pltpu.SemaphoreType.DMA((KV, SUBS)),
                pltpu.SemaphoreType.DMA((2 + SUBS,)),
                pltpu.SemaphoreType.DMA((2 + SUBS,)),
                pltpu.SemaphoreType.DMA((4,)),
                pltpu.SemaphoreType.DMA((SUBS,)),
            ],
            compiler_params=pltpu.CompilerParams(
                collective_id=0, has_side_effects=True, vmem_limit_bytes=(16 + n) * 1024 * 1024
            ),
        )(queries, keys, values, doc_lengths, interp_num, interp_den)

    tokens = P("section", "ctx", None)
    return jax.shard_map(
        on_device,
        mesh=mesh,
        in_specs=(tokens, tokens, tokens, P("section", None), P(), P()),
        out_specs=tokens,
        check_vma=False,
    )
```

```python
from functools import partial
import math

import jax
import jax.numpy as jnp
from jax import lax
from jax.experimental import pallas as pl
from jax.experimental.pallas import tpu as pltpu
from jax.sharding import PartitionSpec as P

HEADS = 32
KV = 4
D = 128
GROUP = HEADS // KV
STACK = 4
SUBS = GROUP // STACK
THETA = 500000.0
MASKED = -1e30
SCALE = math.log2(math.e) / math.sqrt(D)
MESH = pl.DeviceIdType.MESH


def kernel(
    n, sections, q_hbm, k_hbm, v_hbm, len_ref, num_ref, den_ref, out_ref,
    kv, cos_ref, sin_ref, bias_e, bias_l, obuf,
    qbuf, kbuf, vbuf, kv_give, q_give, q_take, len_give, len_take,
    send_sem, recv_sem, osend_sem, orecv_sem, zsend_sem, zrecv_sem, load_sem, store_sem,
):
    me = lax.axis_index("ctx")
    sec = lax.axis_index("section")
    nxt = lax.rem(sec + 1, sections)
    prv = lax.rem(sec + sections - 1, sections)
    chips = n // 2
    chip, core = me // 2, me % 2
    partner = chip * 2 + 1 - core
    rows = qbuf.shape[0]
    half = rows // 2
    last = (KV - 1) * GROUP * D

    loads = [
        pltpu.make_async_copy(k_hbm.at[0], kbuf, load_sem.at[0]),
        pltpu.make_async_copy(v_hbm.at[0], vbuf, load_sem.at[1]),
        pltpu.make_async_copy(
            q_hbm.at[0, :, last:], qbuf.at[:, last:], load_sem.at[2]
        ),
        pltpu.make_async_copy(
            q_hbm.at[0, :, :last], qbuf.at[:, :last], load_sem.at[3]
        ),
    ]
    for load in loads:
        load.start()

    def peer(d):
        return lax.rem(chip + d, chips) * 2 + core

    barrier = pltpu.get_barrier_semaphore()
    for d in range(1, chips):
        pl.semaphore_signal(barrier, inc=1, device_id={"ctx": peer(d)}, device_id_type=MESH)
    pl.semaphore_signal(barrier, inc=1, device_id={"ctx": partner}, device_id_type=MESH)
    pl.semaphore_signal(barrier, inc=1, device_id={"section": nxt}, device_id_type=MESH)
    pl.semaphore_signal(barrier, inc=1, device_id={"section": prv}, device_id_type=MESH)

    r = lax.broadcasted_iota(jnp.int32, (rows, D), 0)
    pos = jnp.where(r < half, me * half + r, (2 * n - 1 - me) * half + r - half)
    def starts(lengths):
        begin = jnp.zeros_like(pos)
        end = jnp.zeros((1, D), jnp.int32)
        for length in lengths:
            end = end + length
            begin = begin + jnp.where(pos >= end, length, 0)
        return begin

    docs = len_ref.shape[1]
    for d in range(docs):
        len_give[d : d + 1, :] = jnp.full((1, D), len_ref[0, d], jnp.int32)
    start = starts([len_give[d : d + 1, :] for d in range(docs)])
    ratio = jnp.full((rows, D), num_ref[0], jnp.int32).astype(jnp.float32) / jnp.full(
        (rows, D), den_ref[0], jnp.int32
    ).astype(jnp.float32)
    lane = lax.broadcasted_iota(jnp.int32, (rows, D), 1)
    k_index = jnp.where(lane < D // 2, lane, lane - D // 2).astype(jnp.float32)
    freq = jnp.exp(k_index * (-2.0 / D * math.log(THETA)))
    angle = (pos - start).astype(jnp.float32) * ratio * freq
    cos = jnp.cos(angle)
    sin = jnp.where(lane < D // 2, -1.0, 1.0) * jnp.sin(angle)
    cos_ref[...] = cos
    sin_ref[...] = sin

    def rotate(x, c, s):
        x = x.astype(jnp.float32)
        return (x * c + pltpu.roll(x, D // 2, 1) * s).astype(jnp.bfloat16)

    def copy(h, shard, slot, to):
        return pltpu.make_async_remote_copy(
            src_ref=kv.at[h, shard],
            dst_ref=kv.at[h, shard],
            send_sem=send_sem.at[h, slot],
            recv_sem=recv_sem.at[h, shard],
            device_id={"ctx": to},
            device_id_type=MESH,
        )

    zpairs = [(kv_give, kv.at[KV - 1, me]), (len_give, len_take)]
    for sub in range(SUBS):
        zpairs.append((q_give.at[sub], q_take.at[sub]))
    zcopies = [
        pltpu.make_async_remote_copy(
            src_ref=src,
            dst_ref=dst,
            send_sem=zsend_sem.at[i],
            recv_sem=zrecv_sem.at[i],
            device_id={"section": nxt},
            device_id_type=MESH,
        )
        for i, (src, dst) in enumerate(zpairs)
    ]

    def push(h):
        for d in range(1, chips):
            copy(h, me, d, peer(d)).start()
        copy(h, me, 0, partner).start()

    loads[0].wait()
    loads[1].wait()
    for h in range(KV):
        cols = slice(h * D, (h + 1) * D)
        turned = rotate(kbuf[:, cols], cos, sin)
        if h == KV - 1:
            kv_give[:, :D] = turned
            kv_give[:, D:] = vbuf[:, cols]
        else:
            kv[h, me, :, :D] = turned
            kv[h, me, :, D:] = vbuf[:, cols]
    pl.semaphore_wait(barrier, chips + 2)
    zcopies[0].start()
    zcopies[1].start()
    push(0)
    loads[2].wait()
    for sub in range(SUBS):
        for g in range(STACK):
            at = last + (sub * STACK + g) * D
            q_give[sub, :, g * D : (g + 1) * D] = rotate(qbuf[:, at : at + D], cos, sin)
        zcopies[2 + sub].start()
    for h in range(1, KV - 1):
        push(h)

    def forward(h):
        for d in range(1, chips):
            shard = peer(chips - d)
            copy(h, shard, chips + d, partner).wait_recv()
            copy(h, shard, chips + d, partner).start()

    keys = n * half

    def set_bias(begin):
        q_pos, q_start = pos[:, :1], begin[:, :1]
        index = lax.broadcasted_iota(jnp.int32, (rows, keys), 1)
        bias_e[...] = jnp.where((index <= q_pos) & (index >= q_start), 0.0, MASKED)
        index = lax.broadcasted_iota(jnp.int32, (half, keys), 1)
        late = (2 * n - 1) * half + lax.rem(index, half) - lax.div(index, half) * half
        seen = (late <= q_pos[half:]) & (late >= q_start[half:])
        bias_l[...] = jnp.where(seen, 0.0, MASKED)

    set_bias(start)
    loads[3].wait()
    forward(0)

    def out_copy(h, sub):
        cols = pl.ds(pl.multiple_of((h * SUBS + sub) * STACK * D, D), STACK * D)
        return pltpu.make_async_remote_copy(
            src_ref=obuf.at[:, cols],
            dst_ref=out_ref.at[0, :, cols],
            send_sem=osend_sem.at[h, sub],
            recv_sem=orecv_sem.at[h, sub],
            device_id={"section": nxt},
            device_id_type=MESH,
        )

    def own_heads(h, sub):
        c, s = cos_ref[...], sin_ref[...]
        base = (h * SUBS + sub) * STACK * D
        return [
            rotate(qbuf[:, pl.ds(pl.multiple_of(base + g * D, D), D)], c, s)
            for g in range(STACK)
        ]

    def attend(h, sub, heads):
        base = (h * SUBS + sub) * STACK * D
        early_kv, late_kv = kv[h, :, :half, :], kv[h, :, half:, :]
        ke = early_kv[:, :, :D].reshape(keys, D)
        kl = late_kv[:, :, :D].reshape(keys, D)
        ones = jnp.ones((keys, D), jnp.bfloat16)
        ve = jnp.concatenate([early_kv[:, :, D:].reshape(keys, D), ones], axis=1)
        vl = jnp.concatenate([late_kv[:, :, D:].reshape(keys, D), ones], axis=1)
        dims = (((1,), (1,)), ((), ()))
        qa = jnp.concatenate(heads, axis=0)
        ql = jnp.concatenate([x[half:] for x in heads], axis=0)
        se = lax.dot_general(qa, ke, dims, preferred_element_type=jnp.float32)
        sl = lax.dot_general(ql, kl, dims, preferred_element_type=jnp.float32)
        se = se.reshape(STACK, rows, keys) + bias_e[...][None]
        sl = sl.reshape(STACK, half, keys) + bias_l[...][None]
        me_ = jnp.max(se, axis=-1, keepdims=True)
        ml = jnp.maximum(jnp.max(sl, axis=-1, keepdims=True), me_[:, half:])
        ma = jnp.concatenate([me_[:, :half], ml], axis=1)
        pe = jnp.exp2((se - ma) * SCALE).astype(jnp.bfloat16).reshape(STACK * rows, keys)
        pL = jnp.exp2((sl - ml) * SCALE).astype(jnp.bfloat16).reshape(STACK * half, keys)
        ae = jnp.dot(pe, ve, preferred_element_type=jnp.float32).reshape(STACK, rows, 2 * D)
        al = jnp.dot(pL, vl, preferred_element_type=jnp.float32).reshape(STACK, half, 2 * D)
        for g in range(STACK):
            cols = pl.ds(pl.multiple_of(base + g * D, D), D)
            top = ae[g, :half]
            low = ae[g, half:] + al[g]
            obuf[:half, cols] = (top[:, :D] / top[:, D:]).astype(jnp.bfloat16)
            obuf[half:, cols] = (low[:, :D] / low[:, D:]).astype(jnp.bfloat16)

    def from_partner(h):
        for d in range(chips):
            shard = lax.rem(chip + d, chips) * 2 + 1 - core
            copy(h, shard, 0, partner).wait_recv()

    def head(h, _):
        from_partner(h)
        attend(h, 0, own_heads(h, 0))
        out_copy(h, 0).start()

        @pl.when(h == 0)
        def _():
            zcopies[0].wait_recv()
            push(KV - 1)

        forward(h + 1)
        for sub in range(1, SUBS):
            attend(h, sub, own_heads(h, sub))
            out_copy(h, sub).start()
        return 0

    lax.fori_loop(0, KV - 1, head, 0)

    zcopies[1].wait_recv()
    set_bias(starts([len_take[d : d + 1, :] for d in range(docs)]))
    from_partner(KV - 1)
    stores = []
    for sub in range(SUBS):
        zcopies[2 + sub].wait_recv()
        heads = [q_take[sub, :, g * D : (g + 1) * D] for g in range(STACK)]
        attend(KV - 1, sub, heads)
        at = last + sub * STACK * D
        cols = slice(at, at + STACK * D)
        store = pltpu.make_async_copy(obuf.at[:, cols], out_ref.at[0, :, cols], store_sem.at[sub])
        store.start()
        stores.append(store)

    def finish(h, _):
        for d in range(2 * chips):
            if d != chips:
                copy(h, me, d, partner).wait_send()
        return 0

    lax.fori_loop(0, KV, finish, 0)
    for store in stores:
        store.wait()
    for zcopy in zcopies:
        zcopy.wait_send()

    def arrive(h, _):
        for sub in range(SUBS):
            out_copy(h, sub).wait_send()
            out_copy(h, sub).wait_recv()
        return 0

    lax.fori_loop(0, KV - 1, arrive, 0)


def solution(mesh):
    n, sections = mesh.shape["ctx"], mesh.shape["section"]

    def on_device(queries, keys, values, doc_lengths, interp_num, interp_den):
        rows = queries.shape[1]
        half = rows // 2
        docs = doc_lengths.shape[1]
        hbm = pl.BlockSpec(memory_space=pltpu.HBM)
        smem = pl.BlockSpec(memory_space=pltpu.SMEM)
        return pl.pallas_call(
            partial(kernel, n, sections),
            out_shape=pltpu.VMEM(queries.shape, jnp.bfloat16),
            in_specs=[hbm, hbm, hbm, smem, smem, smem],
            out_specs=pl.BlockSpec(memory_space=pl.ANY),
            scratch_shapes=[
                pltpu.VMEM((KV, n, rows, 2 * D), jnp.bfloat16),
                pltpu.VMEM((rows, D), jnp.float32),
                pltpu.VMEM((rows, D), jnp.float32),
                pltpu.VMEM((rows, n * half), jnp.float32),
                pltpu.VMEM((half, n * half), jnp.float32),
                pltpu.VMEM((rows, HEADS * D), jnp.bfloat16),
                pltpu.VMEM((rows, HEADS * D), jnp.bfloat16),
                pltpu.VMEM((rows, KV * D), jnp.bfloat16),
                pltpu.VMEM((rows, KV * D), jnp.bfloat16),
                pltpu.VMEM((rows, 2 * D), jnp.bfloat16),
                pltpu.VMEM((SUBS, rows, STACK * D), jnp.bfloat16),
                pltpu.VMEM((SUBS, rows, STACK * D), jnp.bfloat16),
                pltpu.VMEM((docs, D), jnp.int32),
                pltpu.VMEM((docs, D), jnp.int32),
                pltpu.SemaphoreType.DMA((KV, n)),
                pltpu.SemaphoreType.DMA((KV, n)),
                pltpu.SemaphoreType.DMA((KV, SUBS)),
                pltpu.SemaphoreType.DMA((KV, SUBS)),
                pltpu.SemaphoreType.DMA((2 + SUBS,)),
                pltpu.SemaphoreType.DMA((2 + SUBS,)),
                pltpu.SemaphoreType.DMA((4,)),
                pltpu.SemaphoreType.DMA((SUBS,)),
            ],
            compiler_params=pltpu.CompilerParams(
                collective_id=0, has_side_effects=True, vmem_limit_bytes=56*1024*1024
            ),
        )(queries, keys, values, doc_lengths, interp_num, interp_den)

    tokens = P("section", "ctx", None)
    return jax.shard_map(
        on_device,
        mesh=mesh,
        in_specs=(tokens, tokens, tokens, P("section", None), P(), P()),
        out_specs=tokens,
        check_vma=False,
    )
```

```python
from functools import partial
import math

import jax
import jax.numpy as jnp
from jax import lax
from jax.experimental import pallas as pl
from jax.experimental.pallas import tpu as pltpu
from jax.sharding import PartitionSpec as P

HEADS = 32
KV = 4
D = 128
GROUP = HEADS // KV
STACK = 4
SUBS = GROUP // STACK
THETA = 500000.0
MASKED = -1e30
SCALE = math.log2(math.e) / math.sqrt(D)
MESH = pl.DeviceIdType.MESH


def kernel(
    n, sections, q_hbm, k_hbm, v_hbm, len_ref, num_ref, den_ref, out_ref,
    kv, cos_ref, sin_ref, bias_e, bias_l, obuf,
    qbuf, kbuf, vbuf, kv_give, q_take, len_give, len_take,
    send_sem, recv_sem, osend_sem, orecv_sem, zsend_sem, zrecv_sem, load_sem, store_sem,
):
    me = lax.axis_index("ctx")
    sec = lax.axis_index("section")
    nxt = lax.rem(sec + 1, sections)
    prv = lax.rem(sec + sections - 1, sections)
    chips = n // 2
    chip, core = me // 2, me % 2
    partner = chip * 2 + 1 - core
    rows = qbuf.shape[0]
    half = rows // 2
    last = (KV - 1) * GROUP * D

    loads = [
        pltpu.make_async_copy(k_hbm.at[0], kbuf, load_sem.at[0]),
        pltpu.make_async_copy(v_hbm.at[0], vbuf, load_sem.at[1]),
        pltpu.make_async_copy(
            q_hbm.at[0, :, :last], qbuf.at[:, :last], load_sem.at[2]
        ),
    ]
    for load in loads:
        load.start()

    def peer(d):
        return lax.rem(chip + d, chips) * 2 + core

    barrier = pltpu.get_barrier_semaphore()
    for d in range(1, chips):
        pl.semaphore_signal(barrier, inc=1, device_id={"ctx": peer(d)}, device_id_type=MESH)
    pl.semaphore_signal(barrier, inc=1, device_id={"ctx": partner}, device_id_type=MESH)
    pl.semaphore_signal(barrier, inc=1, device_id={"section": nxt}, device_id_type=MESH)
    pl.semaphore_signal(barrier, inc=1, device_id={"section": prv}, device_id_type=MESH)

    zpairs = [(kv_give, kv.at[KV - 1, me]), (len_give, len_take)]
    for sub in range(SUBS):
        at = last + sub * STACK * D
        zpairs.append((q_hbm.at[0, :, at : at + STACK * D], q_take.at[sub]))
    zcopies = [
        pltpu.make_async_remote_copy(
            src_ref=src,
            dst_ref=dst,
            send_sem=zsend_sem.at[i],
            recv_sem=zrecv_sem.at[i],
            device_id={"section": nxt},
            device_id_type=MESH,
        )
        for i, (src, dst) in enumerate(zpairs)
    ]

    pl.semaphore_wait(barrier, chips + 2)
    for sub in range(SUBS):
        zcopies[2 + sub].start()

    r = lax.broadcasted_iota(jnp.int32, (rows, D), 0)
    pos = jnp.where(r < half, me * half + r, (2 * n - 1 - me) * half + r - half)
    def starts(lengths):
        begin = jnp.zeros_like(pos)
        end = jnp.zeros((1, D), jnp.int32)
        for length in lengths:
            end = end + length
            begin = begin + jnp.where(pos >= end, length, 0)
        return begin

    docs = len_ref.shape[1]
    for d in range(docs):
        len_give[d : d + 1, :] = jnp.full((1, D), len_ref[0, d], jnp.int32)
    start = starts([len_give[d : d + 1, :] for d in range(docs)])
    ratio = jnp.full((rows, D), num_ref[0], jnp.int32).astype(jnp.float32) / jnp.full(
        (rows, D), den_ref[0], jnp.int32
    ).astype(jnp.float32)
    lane = lax.broadcasted_iota(jnp.int32, (rows, D), 1)
    k_index = jnp.where(lane < D // 2, lane, lane - D // 2).astype(jnp.float32)
    freq = jnp.exp(k_index * (-2.0 / D * math.log(THETA)))
    def tables(begin):
        angle = (pos - begin).astype(jnp.float32) * ratio * freq
        return jnp.cos(angle), jnp.where(lane < D // 2, -1.0, 1.0) * jnp.sin(angle)

    cos, sin = tables(start)
    cos_ref[...] = cos
    sin_ref[...] = sin

    def rotate(x, c, s):
        x = x.astype(jnp.float32)
        return (x * c + pltpu.roll(x, D // 2, 1) * s).astype(jnp.bfloat16)

    def copy(h, shard, slot, to):
        return pltpu.make_async_remote_copy(
            src_ref=kv.at[h, shard],
            dst_ref=kv.at[h, shard],
            send_sem=send_sem.at[h, slot],
            recv_sem=recv_sem.at[h, shard],
            device_id={"ctx": to},
            device_id_type=MESH,
        )

    def push(h):
        for d in range(1, chips):
            copy(h, me, d, peer(d)).start()
        copy(h, me, 0, partner).start()

    loads[0].wait()
    loads[1].wait()
    for h in range(KV):
        cols = slice(h * D, (h + 1) * D)
        turned = rotate(kbuf[:, cols], cos, sin)
        if h == KV - 1:
            kv_give[:, :D] = turned
            kv_give[:, D:] = vbuf[:, cols]
        else:
            kv[h, me, :, :D] = turned
            kv[h, me, :, D:] = vbuf[:, cols]
    zcopies[0].start()
    zcopies[1].start()
    push(0)
    for h in range(1, KV - 1):
        push(h)

    def forward(h):
        for d in range(1, chips):
            shard = peer(chips - d)
            copy(h, shard, chips + d, partner).wait_recv()
            copy(h, shard, chips + d, partner).start()

    keys = n * half

    def set_bias(begin):
        q_pos, q_start = pos[:, :1], begin[:, :1]
        index = lax.broadcasted_iota(jnp.int32, (rows, keys), 1)
        bias_e[...] = jnp.where((index <= q_pos) & (index >= q_start), 0.0, MASKED)
        index = lax.broadcasted_iota(jnp.int32, (half, keys), 1)
        late = (2 * n - 1) * half + lax.rem(index, half) - lax.div(index, half) * half
        seen = (late <= q_pos[half:]) & (late >= q_start[half:])
        bias_l[...] = jnp.where(seen, 0.0, MASKED)

    set_bias(start)
    loads[2].wait()
    forward(0)

    def out_copy(h, sub):
        cols = pl.ds(pl.multiple_of((h * SUBS + sub) * STACK * D, D), STACK * D)
        return pltpu.make_async_remote_copy(
            src_ref=obuf.at[:, cols],
            dst_ref=out_ref.at[0, :, cols],
            send_sem=osend_sem.at[h, sub],
            recv_sem=orecv_sem.at[h, sub],
            device_id={"section": nxt},
            device_id_type=MESH,
        )

    def own_heads(h, sub):
        c, s = cos_ref[...], sin_ref[...]
        base = (h * SUBS + sub) * STACK * D
        return [
            rotate(qbuf[:, pl.ds(pl.multiple_of(base + g * D, D), D)], c, s)
            for g in range(STACK)
        ]

    def attend(h, sub, heads):
        base = (h * SUBS + sub) * STACK * D
        early_kv, late_kv = kv[h, :, :half, :], kv[h, :, half:, :]
        ke = early_kv[:, :, :D].reshape(keys, D)
        kl = late_kv[:, :, :D].reshape(keys, D)
        ones = jnp.ones((keys, D), jnp.bfloat16)
        ve = jnp.concatenate([early_kv[:, :, D:].reshape(keys, D), ones], axis=1)
        vl = jnp.concatenate([late_kv[:, :, D:].reshape(keys, D), ones], axis=1)
        dims = (((1,), (1,)), ((), ()))
        qa = jnp.concatenate(heads, axis=0)
        ql = jnp.concatenate([x[half:] for x in heads], axis=0)
        se = lax.dot_general(qa, ke, dims, preferred_element_type=jnp.float32)
        sl = lax.dot_general(ql, kl, dims, preferred_element_type=jnp.float32)
        se = se.reshape(STACK, rows, keys) + bias_e[...][None]
        sl = sl.reshape(STACK, half, keys) + bias_l[...][None]
        me_ = jnp.max(se, axis=-1, keepdims=True)
        ml = jnp.maximum(jnp.max(sl, axis=-1, keepdims=True), me_[:, half:])
        ma = jnp.concatenate([me_[:, :half], ml], axis=1)
        pe = jnp.exp2((se - ma) * SCALE).astype(jnp.bfloat16).reshape(STACK * rows, keys)
        pL = jnp.exp2((sl - ml) * SCALE).astype(jnp.bfloat16).reshape(STACK * half, keys)
        ae = jnp.dot(pe, ve, preferred_element_type=jnp.float32).reshape(STACK, rows, 2 * D)
        al = jnp.dot(pL, vl, preferred_element_type=jnp.float32).reshape(STACK, half, 2 * D)
        for g in range(STACK):
            cols = pl.ds(pl.multiple_of(base + g * D, D), D)
            top = ae[g, :half]
            low = ae[g, half:] + al[g]
            obuf[:half, cols] = (top[:, :D] / top[:, D:]).astype(jnp.bfloat16)
            obuf[half:, cols] = (low[:, :D] / low[:, D:]).astype(jnp.bfloat16)

    def from_partner(h):
        for d in range(chips):
            shard = lax.rem(chip + d, chips) * 2 + 1 - core
            copy(h, shard, 0, partner).wait_recv()

    def head(h, _):
        from_partner(h)
        attend(h, 0, own_heads(h, 0))
        out_copy(h, 0).start()

        @pl.when(h == 1)
        def _():
            zcopies[0].wait_recv()
            push(KV - 1)

        forward(h + 1)
        for sub in range(1, SUBS):
            attend(h, sub, own_heads(h, sub))
            out_copy(h, sub).start()
        return 0

    lax.fori_loop(0, KV - 1, head, 0)

    zcopies[1].wait_recv()
    begin = starts([len_take[d : d + 1, :] for d in range(docs)])
    set_bias(begin)
    cos, sin = tables(begin)
    from_partner(KV - 1)
    stores = []
    for sub in range(SUBS):
        zcopies[2 + sub].wait_recv()
        heads = [
            rotate(q_take[sub, :, g * D : (g + 1) * D], cos, sin) for g in range(STACK)
        ]
        attend(KV - 1, sub, heads)
        at = last + sub * STACK * D
        cols = slice(at, at + STACK * D)
        store = pltpu.make_async_copy(obuf.at[:, cols], out_ref.at[0, :, cols], store_sem.at[sub])
        store.start()
        stores.append(store)

    def finish(h, _):
        for d in range(2 * chips):
            if d != chips:
                copy(h, me, d, partner).wait_send()
        return 0

    lax.fori_loop(0, KV, finish, 0)
    for store in stores:
        store.wait()
    for zcopy in zcopies:
        zcopy.wait_send()

    def arrive(h, _):
        for sub in range(SUBS):
            out_copy(h, sub).wait_send()
            out_copy(h, sub).wait_recv()
        return 0

    lax.fori_loop(0, KV - 1, arrive, 0)


def solution(mesh):
    n, sections = mesh.shape["ctx"], mesh.shape["section"]

    def on_device(queries, keys, values, doc_lengths, interp_num, interp_den):
        rows = queries.shape[1]
        half = rows // 2
        docs = doc_lengths.shape[1]
        hbm = pl.BlockSpec(memory_space=pltpu.HBM)
        smem = pl.BlockSpec(memory_space=pltpu.SMEM)
        return pl.pallas_call(
            partial(kernel, n, sections),
            out_shape=pltpu.VMEM(queries.shape, jnp.bfloat16),
            in_specs=[hbm, hbm, hbm, smem, smem, smem],
            out_specs=pl.BlockSpec(memory_space=pl.ANY),
            scratch_shapes=[
                pltpu.VMEM((KV, n, rows, 2 * D), jnp.bfloat16),
                pltpu.VMEM((rows, D), jnp.float32),
                pltpu.VMEM((rows, D), jnp.float32),
                pltpu.VMEM((rows, n * half), jnp.float32),
                pltpu.VMEM((half, n * half), jnp.float32),
                pltpu.VMEM((rows, HEADS * D), jnp.bfloat16),
                pltpu.VMEM((rows, HEADS * D), jnp.bfloat16),
                pltpu.VMEM((rows, KV * D), jnp.bfloat16),
                pltpu.VMEM((rows, KV * D), jnp.bfloat16),
                pltpu.VMEM((rows, 2 * D), jnp.bfloat16),
                pltpu.VMEM((SUBS, rows, STACK * D), jnp.bfloat16),
                pltpu.VMEM((docs, D), jnp.int32),
                pltpu.VMEM((docs, D), jnp.int32),
                pltpu.SemaphoreType.DMA((KV, n)),
                pltpu.SemaphoreType.DMA((KV, n)),
                pltpu.SemaphoreType.DMA((KV, SUBS)),
                pltpu.SemaphoreType.DMA((KV, SUBS)),
                pltpu.SemaphoreType.DMA((2 + SUBS,)),
                pltpu.SemaphoreType.DMA((2 + SUBS,)),
                pltpu.SemaphoreType.DMA((3,)),
                pltpu.SemaphoreType.DMA((SUBS,)),
            ],
            compiler_params=pltpu.CompilerParams(
                collective_id=0, has_side_effects=True, vmem_limit_bytes=56*1024*1024
            ),
        )(queries, keys, values, doc_lengths, interp_num, interp_den)

    tokens = P("section", "ctx", None)
    return jax.shard_map(
        on_device,
        mesh=mesh,
        in_specs=(tokens, tokens, tokens, P("section", None), P(), P()),
        out_specs=tokens,
        check_vma=False,
    )
```
